256 devices in a mesh: ctx: 32 (over x, z), dp: 8 (over y, core).
Axes of the slice: x: 4, y: 4, z: 8, core: 2. Of those that a mesh axis runs over, the one named last changes fastest.
Arguments:
- queries: bfloat16 [8, 4096, 4096], P('dp', 'ctx'), may hold values from -25 to 25
- key_rows: bfloat16 [8, 4096, 4096], P('dp', 'ctx'), may hold values from -25 to 25
- values: bfloat16 [8, 4096, 4096], P('dp', 'ctx'), may hold values from -6 to 6
- upstream: bfloat16 [8, 4096, 2048], P('dp', 'ctx'), may hold values from -6 to 6
- out_weight: bfloat16 [4096, 2048], P('ctx', 'dp'), may hold values from -0.125 to 0.125
- doc_lengths: int32 [8, 2, 8], P('dp'), may hold values from 1 to 1024, 2048 in all within a row
Outputs:
- grad_queries: bfloat16 [8, 4096, 4096], P('dp', 'ctx')
- grad_keys: bfloat16 [8, 4096, 4096], P('dp', 'ctx')
- grad_values: bfloat16 [8, 4096, 4096], P('dp', 'ctx')
- grad_out_weight: float32 [4096, 2048], P('ctx', 'dp')
The draws below stay inside these ranges and needn't reach their ends.
Inputs may be any that keep to these rules, and one draw needn't show every extreme that they name: `doc_lengths`: each sequence's 8 lengths sum to 2048, and the largest of them is exactly 1024.
All inputs are finite; a program needn't handle non-finite values.
Results may differ from the reference program's by a relative error of at most 0.017.
Values may be sent and summed in bfloat16 or wider, within the bound.
No kernel may reach another device: no remote copies, remote signals or barrier semaphores. Data moves between devices by JAX's collectives and lax.ppermute only.
A program may use at most 256 MiB of HBM per device.

```python
import math
import jax
import jax.numpy as jnp
import numpy as np
from jax import lax

H = 32
HD = 128
D_WIN = 2048
SEQS = 2
DOCS = 8
GROUP_TOKENS = 4096
SEQ_LEN = 2048
N_DP = 8


def draw_queries(key, part):
    key = jax.random.fold_in(key, 1)
    shape = (N_DP, GROUP_TOKENS, H * HD)
    return jax.random.truncated_normal(key, -4.0, 4.0, shape, jnp.float32).astype(jnp.bfloat16)


def draw_key_rows(key, part):
    key = jax.random.fold_in(key, 2)
    shape = (N_DP, GROUP_TOKENS, H * HD)
    return jax.random.truncated_normal(key, -4.0, 4.0, shape, jnp.float32).astype(jnp.bfloat16)


def block_scale(own_key, extent, shards, low, high):
    factor_of = 1.0
    for axis_at, shards_of in shards:
        steps = jax.random.uniform(jax.random.fold_in(jax.random.fold_in(own_key, 6), axis_at), (shards_of,), jnp.float32, low / len(shards), high / len(shards))
        factor_of = factor_of * jnp.repeat(jnp.exp(steps), extent[axis_at] // shards_of).reshape((-1,) + (1,) * (len(extent) - 1 - axis_at))
    return factor_of


def split_up(amount, total, limit, slope):
    portions = [(1 << 20) // math.isqrt(grade ** slope) + 1 for grade in range(2, amount + 1)]
    spare, holding = total - limit - (amount - 1), [1] * (amount - 1)
    while spare > 0:
        candidates = [i for i in range(amount - 1) if holding[i] < limit]
        mass, budget = sum([portions[i] for i in candidates]), spare
        for i in candidates:
            addition = min(limit - holding[i], max(1, budget * portions[i] // mass), spare)
            holding[i] = holding[i] + addition
            spare = spare - addition
    return np.array([limit] + holding)


def uneven_parts(key, amount, total, limit, lean):
    if amount == 2:
        one = jax.random.randint(key, (), max(1, total - limit), min(limit, total - 1) + 1)
        return jnp.stack([one, total - one])
    sizes = jnp.asarray(split_up(amount, total, limit, lean), jnp.int32)
    twos = (amount - 1) // 2
    source_of, sink = sizes[1:1 + 2 * twos:2], sizes[2:2 + 2 * twos:2]
    room = jnp.minimum(source_of - 1, limit - sink)
    shifted = jax.random.randint(jax.random.fold_in(key, 1), (twos,), 0, 1 << 20) % (room + 1)
    sizes = sizes.at[1:1 + 2 * twos:2].set(source_of - shifted).at[2:2 + 2 * twos:2].set(sink + shifted)
    return sizes[jax.random.permutation(jax.random.fold_in(key, 2), amount)]


def gaussian(key, shape, deviation, bound, pieces=(), kind=jnp.bfloat16):
    level = block_scale(key, shape, pieces, -0.22, 0.18) if pieces else 1.0
    array = jax.random.normal(key, shape, jnp.float32) * deviation * level
    return jnp.minimum(jnp.maximum(array, -bound), bound).astype(kind)


def setup_inputs(seed: int = 0) -> dict:
    streams_of = jax.random.split(jax.random.key(seed), 7)
    return {
        "queries": draw_queries(jax.random.fold_in(streams_of[6], 71), 0),
        "key_rows": draw_key_rows(jax.random.fold_in(streams_of[6], 71), 0),
        "values": gaussian(streams_of[2], (N_DP, GROUP_TOKENS, H * HD), 1.0, 6.0, ((0, 8), (1, 32))),
        "upstream": gaussian(streams_of[3], (N_DP, GROUP_TOKENS, D_WIN), 1.0, 6.0, ((0, 8), (1, 32))),
        "out_weight": gaussian(streams_of[4], (H * HD, D_WIN), D_WIN ** -0.5, 0.125, ((0, 32), (1, 8))),
        "doc_lengths": jax.vmap(lambda own: uneven_parts(own, DOCS, SEQ_LEN, SEQ_LEN // 2, 2))(jax.random.split(streams_of[5], N_DP * SEQS)).reshape((N_DP, SEQS, DOCS)).astype(jnp.int32),
    }


def document_ids(lengths, seq_span):
    bounds = jnp.cumsum(lengths, axis=-1)
    places = jnp.arange(seq_span, dtype=jnp.int32)
    return jnp.sum((places[None, :, None] >= bounds[:, None, :]).astype(jnp.int32), axis=-1)


def forward_sequence(query_rows, key_part, value_part, doc_ids):
    factor = query_rows.shape[-1] ** -0.5
    same_doc = doc_ids[:, None] == doc_ids[None, :]
    scores = jnp.einsum("qhd,khd->hqk", query_rows.astype(jnp.float32), key_part.astype(jnp.float32)) * factor
    scores = jnp.where(same_doc[None], scores, -jnp.inf)
    row_max = jnp.max(scores, axis=-1, keepdims=True)
    expo = jnp.exp(scores - row_max)
    probs = expo / jnp.sum(expo, axis=-1, keepdims=True)
    probs_low = lax.optimization_barrier(probs.astype(jnp.bfloat16)).astype(jnp.float32)
    attn_out = jnp.einsum("hqk,khd->qhd", probs_low, value_part.astype(jnp.float32)).astype(jnp.bfloat16)
    return probs, attn_out


def backward_sequence(query_rows, key_part, value_part, probs, attn_out, grad_attn):
    factor = query_rows.shape[-1] ** -0.5
    probs_low = lax.optimization_barrier(probs.astype(jnp.bfloat16)).astype(jnp.float32)
    grad_f = grad_attn.astype(jnp.float32)
    grad_value = jnp.einsum("hqk,qhd->khd", probs_low, grad_f).astype(jnp.bfloat16)
    grad_probs = jnp.einsum("qhd,khd->hqk", grad_f, value_part.astype(jnp.float32))
    delta = jnp.sum(grad_f * attn_out.astype(jnp.float32), axis=-1)
    grad_scores = probs * (grad_probs - jnp.transpose(delta)[:, :, None])
    grad_low = lax.optimization_barrier(grad_scores.astype(jnp.bfloat16)).astype(jnp.float32)
    grad_query = (jnp.einsum("hqk,khd->qhd", grad_low, key_part.astype(jnp.float32)) * factor).astype(jnp.bfloat16)
    grad_key = (jnp.einsum("hqk,qhd->khd", grad_low, query_rows.astype(jnp.float32)) * factor).astype(jnp.bfloat16)
    return grad_query, grad_key, grad_value


def reference(queries, key_rows, values, upstream, out_weight, doc_lengths):
    feat_width = H * HD

    def one_group(weight_total, members):
        query_grp, key_grp, value_grp, upstream_grp, lengths_grp = members
        doc_ids = document_ids(lengths_grp, SEQ_LEN)

        def split(arr):
            return arr.reshape(SEQS, SEQ_LEN, H, HD)

        probs, attn_out = lax.map(lambda members_seq: forward_sequence(*members_seq), (split(query_grp), split(key_grp), split(value_grp), doc_ids))
        flat_out = attn_out.reshape(GROUP_TOKENS, feat_width)
        grad_attn = jnp.dot(upstream_grp, out_weight.T, preferred_element_type=jnp.float32).astype(jnp.bfloat16)
        weight_total = weight_total + jnp.dot(flat_out.T, upstream_grp, preferred_element_type=jnp.float32)
        grads = lax.map(lambda members_seq: backward_sequence(*members_seq), (split(query_grp), split(key_grp), split(value_grp), probs, attn_out, split(grad_attn)))
        grads = tuple(item.reshape(GROUP_TOKENS, feat_width) for item in grads)
        return weight_total, grads

    start_total = jnp.zeros((feat_width, D_WIN), jnp.float32)
    weight_total, grads = lax.scan(one_group, start_total, (queries, key_rows, values, upstream, doc_lengths))
    return grads[0], grads[1], grads[2], weight_total
```

```python
import functools

import jax
import jax.numpy as jnp
from jax import lax
from jax.experimental import pallas as pl
from jax.experimental.pallas import tpu as pltpu
from jax.sharding import Mesh, PartitionSpec as P

HD = 128
SEQS = 2
ZN = 8
TILE = 128
SEQ = 2048
HALF = SEQ // 2
BLK = 512
SHIFT = 9
NBLK = SEQ // BLK
SWAP = [(0, 1), (1, 0)]
TRANSPOSE = [(0, 0), (1, 2), (2, 1), (3, 3)]
LOW = -1e30
VMEM_LIMIT = 48 * 1024 * 1024


def params():
    return pltpu.CompilerParams(vmem_limit_bytes=VMEM_LIMIT)


def matmul(lhs, rhs, left, right):
    return lax.dot_general(
        lhs, rhs, (((left,), (right,)), ((), ())), preferred_element_type=jnp.float32
    )


def pack_kernel(q_ref, k_ref, v_ref, out_ref):
    for z in range(ZN):
        for t, ref in enumerate((q_ref, k_ref, v_ref)):
            out_ref[z, 0, t * TILE : (t + 1) * TILE, :] = ref[0, :, z * HD : (z + 1) * HD]


def pack(queries, keys, values, chunk):
    rows = pl.BlockSpec((1, TILE, ZN * HD), lambda c: (0, 0, 2 * c + chunk))
    return pl.pallas_call(
        pack_kernel,
        grid=(2,),
        in_specs=[rows] * 3,
        out_specs=pl.BlockSpec((ZN, 1, 3 * TILE, HD), lambda c: (0, c, 0, 0)),
        out_shape=jax.ShapeDtypeStruct((ZN, 2, 3 * TILE, HD), jnp.bfloat16),
        compiler_params=params(),
        name=f"pack{chunk}",
    )(queries, keys, values)


def unpack_kernel(in_ref, *refs):
    for z in range(ZN):
        for t, ref in enumerate(refs[-3:]):
            ref[0, :, z * HD : (z + 1) * HD] = in_ref[z, 0, t * TILE : (t + 1) * TILE, :]


def unpack(blocks, chunk, held):
    rows = pl.BlockSpec((1, TILE, ZN * HD), lambda c: (0, 0, 2 * c + chunk))
    whole = jax.ShapeDtypeStruct((1, TILE, 4 * ZN * HD), jnp.bfloat16)
    return pl.pallas_call(
        unpack_kernel,
        grid=(2,),
        in_specs=[pl.BlockSpec((ZN, 1, 3 * TILE, HD), lambda c: (0, c, 0, 0))]
        + [pl.BlockSpec(memory_space=pl.ANY)] * len(held),
        out_specs=[rows] * 3,
        out_shape=[whole] * 3,
        input_output_aliases={i + 1: i for i in range(len(held))},
        compiler_params=params(),
        name=f"unpack{chunk}",
    )(blocks, *held)


def put_kernel(info_ref, in_ref, held_ref, out_ref):
    out_ref[...] = in_ref[...]


def put_other(info, part, blocks):
    return pl.pallas_call(
        put_kernel,
        grid_spec=pltpu.PrefetchScalarGridSpec(
            num_scalar_prefetch=1,
            grid=(1,),
            in_specs=[
                pl.BlockSpec((ZN, 1, 3 * TILE, HD), lambda i, info: (0, 0, 0, 0)),
                pl.BlockSpec(memory_space=pl.ANY),
            ],
            out_specs=pl.BlockSpec((ZN, 1, 3 * TILE, HD), lambda i, info: (0, 1 - info[0], 0, 0)),
        ),
        out_shape=jax.ShapeDtypeStruct((ZN, 2, 3 * TILE, HD), jnp.bfloat16),
        input_output_aliases={2: 0},
        compiler_params=params(),
        name="put",
    )(info, part, blocks)


def attend_kernel(
    info, left, right, g, *refs
):
    *grads_out, o_out, q_s, k_s, v_s, g_s, kt_s, vt_s, p_s, dq_s, dk_s, dv_s = refs
    factor = HD ** (-0.5)
    for z in range(ZN):
        for t, ref in enumerate((q_s, k_s, v_s)):
            for c, part in enumerate((left, right)):
                row = c * HALF + z * TILE
                ref[row : row + TILE, :] = part[z, 0, t * TILE : (t + 1) * TILE, :]
        for c in range(2):
            g_s[c * HALF + z * TILE : c * HALF + (z + 1) * TILE, :] = g[z, c]
    for j in range(NBLK):
        kt_s[j] = k_s[j * BLK : (j + 1) * BLK, :].T
        vt_s[j] = v_s[j * BLK : (j + 1) * BLK, :].T
    dk_s[...] = jnp.zeros_like(dk_s)
    dv_s[...] = jnp.zeros_like(dv_s)
    bounds = [info[1 + d] for d in range(7)]

    def query_block(i, carry):
        base = pl.multiple_of(i * BLK, BLK)
        q_i = q_s[pl.ds(base, BLK), :]
        g_i = g_s[pl.ds(base, BLK), :]
        place = base + lax.broadcasted_iota(jnp.int32, (1, BLK), 1)
        start, end = jnp.zeros_like(place), jnp.full_like(place, SEQ)
        first, last = jnp.int32(0), jnp.int32(SEQ)
        for bound in bounds:
            start = jnp.where(place >= bound, bound, start)
            first = jnp.where(base >= bound, bound, first)
        for bound in bounds[::-1]:
            end = jnp.where(place < bound, bound, end)
            last = jnp.where(base + BLK - 1 < bound, bound, last)
        lo = lax.shift_right_logical(first, SHIFT)
        hi = lax.shift_right_logical(last + BLK - 1, SHIFT)

        def score(j, top):
            rows = pl.multiple_of(j * BLK, BLK)
            s = matmul(k_s[pl.ds(rows, BLK), :], q_i, 1, 1) * factor
            seen = rows + lax.broadcasted_iota(jnp.int32, (BLK, BLK), 0)
            s = jnp.where((seen >= start) & (seen < end), s, LOW)
            p_s[j] = s
            return jnp.maximum(top, jnp.max(s, axis=0, keepdims=True))

        top = lax.fori_loop(lo, hi, score, jnp.full((1, BLK), LOW, jnp.float32))

        def mix(j, held):
            total, out = held
            p = jnp.exp(p_s[j] - top)
            p_s[j] = p
            total = total + jnp.sum(p, axis=0, keepdims=True)
            return total, out + matmul(vt_s[j], p.astype(jnp.bfloat16), 1, 0)

        total, out = lax.fori_loop(
            lo, hi, mix, (jnp.zeros((1, BLK), jnp.float32), jnp.zeros((HD, BLK), jnp.float32))
        )
        inverse = 1.0 / total
        out = (out * inverse).astype(jnp.bfloat16).astype(jnp.float32)
        g_t = g_i.astype(jnp.float32).T
        delta = jnp.sum(g_t * out, axis=0, keepdims=True)
        out_rows = out.T.astype(jnp.bfloat16)
        side, tile = lax.shift_right_logical(i, 1), 4 * lax.bitwise_and(i, 1)
        for n in range(BLK // TILE):
            o_out[tile + n, side] = out_rows[n * TILE : (n + 1) * TILE]

        def grads(j, dq_t):
            rows = pl.multiple_of(j * BLK, BLK)
            probs = p_s[j] * inverse
            grad_p = matmul(v_s[pl.ds(rows, BLK), :], g_i, 1, 1)
            grad_s = (probs * (grad_p - delta)).astype(jnp.bfloat16)
            dv_s[pl.ds(rows, BLK), :] += matmul(probs.astype(jnp.bfloat16), g_i, 1, 0)
            dk_s[pl.ds(rows, BLK), :] += matmul(grad_s, q_i, 1, 0)
            return dq_t + matmul(kt_s[j], grad_s, 1, 0)

        dq_t = lax.fori_loop(lo, hi, grads, jnp.zeros((HD, BLK), jnp.float32))
        dq_s[pl.ds(base, BLK), :] = (dq_t * factor).T.astype(jnp.bfloat16)
        return carry

    lax.fori_loop(0, NBLK, query_block, 0)
    halves = (0, 1) if len(grads_out) == 1 else (info[0], 1 - info[0])
    for n, half in enumerate(halves):
        ref, side = (grads_out[0], n) if len(grads_out) == 1 else (grads_out[n], 0)
        for z in range(ZN):
            rows = pl.ds(pl.multiple_of(half * HALF + z * TILE, TILE), TILE)
            ref[z, side, :TILE, :] = dq_s[rows, :]
            ref[z, side, TILE : 2 * TILE, :] = (dk_s[rows, :] * factor).astype(jnp.bfloat16)
            ref[z, side, 2 * TILE :, :] = dv_s[rows, :].astype(jnp.bfloat16)


def attend(info, blocks, grad_attn, chunk):
    flat = (SEQ, HD)
    whole, half = (ZN, 2, 3 * TILE, HD), (ZN, 1, 3 * TILE, HD)
    if chunk == 0:
        specs = [pl.BlockSpec(whole, lambda i, info: (0, 0, 0, 0))]
        shapes = [whole]
    else:
        specs = [
            pl.BlockSpec(half, lambda i, info: (0, info[0], 0, 0)),
            pl.BlockSpec(half, lambda i, info: (0, 0, 0, 0)),
        ]
        shapes = [whole, half]
    return pl.pallas_call(
        attend_kernel,
        grid_spec=pltpu.PrefetchScalarGridSpec(
            num_scalar_prefetch=1,
            grid=(1,),
            in_specs=[
                pl.BlockSpec(half, lambda i, info: (0, 0, 0, 0)),
                pl.BlockSpec(half, lambda i, info: (0, 1, 0, 0)),
                pl.BlockSpec((ZN, 2, TILE, HD), lambda i, info: (0, 0, 0, chunk)),
            ],
            out_specs=specs + [pl.BlockSpec((ZN, 2, TILE, HD), lambda i, info: (0, 0, 0, 0))],
            scratch_shapes=[pltpu.VMEM(flat, jnp.bfloat16)] * 4
            + [pltpu.VMEM((NBLK, HD, BLK), jnp.bfloat16)] * 2
            + [pltpu.VMEM((NBLK, BLK, BLK), jnp.float32)]
            + [pltpu.VMEM(flat, jnp.bfloat16)]
            + [pltpu.VMEM(flat, jnp.float32)] * 2,
        ),
        out_shape=[jax.ShapeDtypeStruct(s, jnp.bfloat16) for s in shapes + [(ZN, 2, TILE, HD)]],
        compiler_params=params(),
        cost_estimate=pl.CostEstimate(
            flops=12 * SEQ * SEQ * HD, bytes_accessed=8 << 20, transcendentals=SEQ * SEQ
        ),
        name=f"attend{chunk}",
    )(info, blocks, blocks, grad_attn)


def project_kernel(rows_ref, weight_ref, out_ref):
    out = matmul(rows_ref[...], weight_ref[...], 1, 1).astype(jnp.bfloat16)
    for n in range(out.shape[0] // TILE):
        out_ref[n // 2, n % 2] = out[n * TILE : (n + 1) * TILE]


def project(rows, weights):
    width = rows.shape[1]
    return pl.pallas_call(
        project_kernel,
        grid=(SEQ // BLK,),
        in_specs=[
            pl.BlockSpec((BLK, width), lambda i: (i, 0)),
            pl.BlockSpec((2 * HD, width), lambda i: (0, 0)),
        ],
        out_specs=pl.BlockSpec((BLK // TILE // 2, 2, TILE, 2 * HD), lambda i: (i, 0, 0, 0)),
        out_shape=jax.ShapeDtypeStruct((ZN, 2, TILE, 2 * HD), jnp.bfloat16),
        compiler_params=params(),
        cost_estimate=pl.CostEstimate(
            flops=4 * SEQ * HD * width, bytes_accessed=10 << 20, transcendentals=0
        ),
        name="project",
    )(rows, weights)


def exchange(blocks):
    flat = blocks.reshape(2 * ZN, 3 * TILE, HD)
    moved = lax.all_to_all(flat, ("z", "c"), split_axis=0, concat_axis=0, tiled=True)
    return moved.reshape(blocks.shape)


def sum_planes(term):
    y = lax.axis_index("y")
    low, high = lax.bitwise_and(y, 1) == 0, y < 2
    parts = [term[:, i * 512 : (i + 1) * 512] for i in range(4)]
    even = jnp.concatenate([parts[0], parts[2]], axis=1)
    odd = jnp.concatenate([parts[1], parts[3]], axis=1)
    send = jnp.where(low, odd, even).astype(jnp.bfloat16)
    got = lax.ppermute(send, "y", [(0, 1), (1, 0), (2, 3), (3, 2)])
    both = jnp.where(low, even, odd) + got.astype(jnp.float32)
    send = jnp.where(high, both[:, 512:], both[:, :512]).astype(jnp.bfloat16)
    got = lax.ppermute(send, "y", [(0, 2), (2, 0), (1, 3), (3, 1)])
    return jnp.where(high, both[:, :512], both[:, 512:]) + got.astype(jnp.float32)


def swap(array):
    return lax.ppermute(array, ("xh", "c"), TRANSPOSE)


def on_device(queries, key_rows, values, upstream, out_weight, doc_lengths):
    xs, xh = lax.axis_index("xs"), lax.axis_index("xh")
    group_rows = swap(upstream[0])
    tok_rows = lax.all_gather(group_rows, ("z", "c"), axis=0, tiled=True)

    first = pack(queries, key_rows, values, 0)
    first, group_rows = lax.optimization_barrier((first, group_rows))
    first = swap(first)

    weight = lax.all_gather(out_weight, ("y", "c"), axis=1, tiled=True)
    first, weight = lax.optimization_barrier((first, weight))
    first = exchange(first)

    second = swap(pack(queries, key_rows, values, 1))
    second, weight = lax.optimization_barrier((second, weight))
    weight = lax.ppermute(weight, ("xs", "c"), TRANSPOSE)
    other_weight = lax.ppermute(weight, "xh", SWAP)
    weights = jnp.concatenate(
        [jnp.where(xh == 0, weight, other_weight), jnp.where(xh == 0, other_weight, weight)]
    )
    lengths = lax.dynamic_index_in_dim(doc_lengths[0], xs, 0, keepdims=False)
    info = jnp.concatenate([xh.astype(jnp.int32)[None], jnp.cumsum(swap(lengths))])
    second, first, weights, info = lax.optimization_barrier((second, first, weights, info))
    second = exchange(second)

    grad_attn = project(tok_rows, weights)
    grads, out_one = attend(info, first, grad_attn, 0)
    grads, second = lax.optimization_barrier((grads, second))
    grads = exchange(grads)
    near, far, out_two = attend(info, second, grad_attn, 1)
    back = put_other(info, lax.ppermute(far, "xh", SWAP), near)
    terms = [
        jnp.einsum("tf,tc->fc", out.reshape(SEQ, HD), tok_rows, preferred_element_type=jnp.float32)
        for out in (out_two, out_one)
    ]
    back, grads, terms = lax.optimization_barrier((back, grads, terms))
    back = exchange(back)
    sums = [sum_planes(term) for term in terms[::-1]]

    send = jnp.where(xh == 0, sums[1], sums[0]).astype(jnp.bfloat16)
    total = jnp.where(xh == 0, sums[0], sums[1]) + lax.ppermute(send, "xh", SWAP).astype(jnp.float32)
    grads, total = lax.optimization_barrier((grads, total))
    held = unpack(swap(grads), 0, ())
    held = unpack(back, 1, held)
    one, two = total[:, :256], total[:, 256:]
    straight = lax.ppermute(jnp.where(xs == 0, one, two), ("xs", "c"), TRANSPOSE)
    crossed = lax.ppermute(
        jnp.where(xs == 0, two, one), ("xs", "c"), [(0, 1), (1, 3), (2, 0), (3, 2)]
    )
    return (*held, straight + crossed)


def solution(mesh):
    fine = Mesh(mesh.devices.reshape(2, 2, ZN, 4, 2), ("xs", "xh", "z", "y", "c"))
    ctx, dp = ("xs", "xh", "z"), ("y", "c")
    rows = P(dp, ctx, None)
    return jax.shard_map(
        on_device,
        mesh=fine,
        in_specs=(rows, rows, rows, rows, P(ctx, dp), P(dp, None, None)),
        out_specs=(rows, rows, rows, P(ctx, dp)),
        check_vma=False,
    )
```

```python
import jax
import jax.numpy as jnp
from jax import lax
from jax.experimental import pallas as pl
from jax.experimental.pallas import tpu as pltpu
from jax.sharding import Mesh, PartitionSpec as P

HD = 128
SEQS = 2
ZN = 8
TILE = 128
SEQ = 2048
HALF = SEQ // 2
BLK = 512
SWAP = [(0, 1), (1, 0)]
TRANSPOSE = [(0, 0), (1, 2), (2, 1), (3, 3)]
LOW = -1e30
VMEM_LIMIT = 48 * 1024 * 1024


def params():
    return pltpu.CompilerParams(vmem_limit_bytes=VMEM_LIMIT)


def matmul(lhs, rhs, left, right):
    return lax.dot_general(
        lhs, rhs, (((left,), (right,)), ((), ())), preferred_element_type=jnp.float32
    )


def pack_kernel(q_ref, k_ref, v_ref, out_ref):
    for z in range(ZN):
        for t, ref in enumerate((q_ref, k_ref, v_ref)):
            out_ref[z, 0, t * TILE : (t + 1) * TILE, :] = ref[0, :, z * HD : (z + 1) * HD]


def pack(queries, keys, values, chunk):
    rows = pl.BlockSpec((1, TILE, ZN * HD), lambda c: (0, 0, 2 * c + chunk))
    return pl.pallas_call(
        pack_kernel,
        grid=(2,),
        in_specs=[rows] * 3,
        out_specs=pl.BlockSpec((ZN, 1, 3 * TILE, HD), lambda c: (0, c, 0, 0)),
        out_shape=jax.ShapeDtypeStruct((ZN, 2, 3 * TILE, HD), jnp.bfloat16),
        compiler_params=params(),
        name=f"pack{chunk}",
    )(queries, keys, values)


def unpack_kernel(in_ref, *refs):
    for z in range(ZN):
        for t, ref in enumerate(refs[-3:]):
            ref[0, :, z * HD : (z + 1) * HD] = in_ref[z, 0, t * TILE : (t + 1) * TILE, :]


def unpack(blocks, chunk, held):
    rows = pl.BlockSpec((1, TILE, ZN * HD), lambda c: (0, 0, 2 * c + chunk))
    whole = jax.ShapeDtypeStruct((1, TILE, 4 * ZN * HD), jnp.bfloat16)
    return pl.pallas_call(
        unpack_kernel,
        grid=(2,),
        in_specs=[pl.BlockSpec((ZN, 1, 3 * TILE, HD), lambda c: (0, c, 0, 0))]
        + [pl.BlockSpec(memory_space=pl.ANY)] * len(held),
        out_specs=[rows] * 3,
        out_shape=[whole] * 3,
        input_output_aliases={i + 1: i for i in range(len(held))},
        compiler_params=params(),
        name=f"unpack{chunk}",
    )(blocks, *held)


def put_kernel(info_ref, in_ref, held_ref, out_ref):
    out_ref[...] = in_ref[...]


def put_other(info, part, blocks):
    return pl.pallas_call(
        put_kernel,
        grid_spec=pltpu.PrefetchScalarGridSpec(
            num_scalar_prefetch=1,
            grid=(1,),
            in_specs=[
                pl.BlockSpec((ZN, 1, 3 * TILE, HD), lambda i, info: (0, 0, 0, 0)),
                pl.BlockSpec(memory_space=pl.ANY),
            ],
            out_specs=pl.BlockSpec((ZN, 1, 3 * TILE, HD), lambda i, info: (0, 1 - info[0], 0, 0)),
        ),
        out_shape=jax.ShapeDtypeStruct((ZN, 2, 3 * TILE, HD), jnp.bfloat16),
        input_output_aliases={2: 0},
        compiler_params=params(),
        name="put",
    )(info, part, blocks)


def attend_kernel(info, one, two, g, *refs):
    *grads_out, o_out, q_s, k_s, v_s, g_s, kt_s, vt_s, b_q, b_k, b_v, b_o = refs
    factor = HD ** (-0.5)
    shift = info[1]
    tiles = SEQ // TILE
    sides = (info[0], 1 - info[0])
    out_sides = (0, 1) if len(grads_out) == 1 else sides

    def wrap(row):
        return jnp.where(row < 0, row + SEQ, jnp.where(row >= SEQ, row - SEQ, row))

    def repeat(buf):
        buf[SEQ:, :] = buf[:TILE, :]

    for side, part in enumerate((one, two)):
        for z in range(ZN):
            rows = slice(side * HALF + z * TILE, side * HALF + (z + 1) * TILE)
            for t, buf in enumerate((b_q, b_k, b_v)):
                buf[rows, :] = part[z, 0, t * TILE : (t + 1) * TILE, :].astype(jnp.float32)
    for z in range(ZN):
        for c in range(2):
            row = c * HALF + z * TILE
            b_o[row : row + TILE, :] = g[z, c].astype(jnp.float32)
    for buf, ref in ((b_q, q_s), (b_k, k_s), (b_v, v_s), (b_o, g_s)):
        repeat(buf)
        for j in range(tiles):
            rows = pl.ds(wrap(shift + j * TILE), TILE)
            ref[j * TILE : (j + 1) * TILE, :] = buf[rows, :].astype(jnp.bfloat16)
    for n in range(2):
        kt_s[n] = k_s[n * HALF : (n + 1) * HALF, :].T
        vt_s[n] = v_s[n * HALF : (n + 1) * HALF, :].T
    b_k[...] = jnp.zeros_like(b_k)
    b_v[...] = jnp.zeros_like(b_v)
    ends = [wrap(info[2 + d] - shift) for d in range(8)]

    for n in range(2):
        low = n * HALF
        keys = slice(low, low + HALF)

        def query_block(i, carry):
            rows = pl.ds(pl.multiple_of(low + i * BLK, BLK), BLK)
            q_i, g_i = q_s[rows, :], g_s[rows, :]
            s = matmul(k_s[keys, :], q_i, 1, 1)
            if n == 1:
                place = low + i * BLK + lax.broadcasted_iota(jnp.int32, (1, BLK), 1)
                start, stop = jnp.full_like(place, HALF), jnp.full_like(place, SEQ)
                for end in ends:
                    start = jnp.maximum(start, jnp.where(end <= place, end, HALF))
                    stop = jnp.minimum(stop, jnp.where(end > place, end, SEQ))
                seen = low + lax.broadcasted_iota(jnp.int32, (HALF, BLK), 0)
                s = jnp.where((seen >= start) & (seen < stop), s, LOW)
            top = jnp.max(s, axis=0, keepdims=True)
            probs = jnp.exp((s - top) * factor)
            probs = probs * (1.0 / jnp.sum(probs, axis=0, keepdims=True))
            probs_low = probs.astype(jnp.bfloat16)
            out = matmul(vt_s[n], probs_low, 1, 0).astype(jnp.bfloat16).astype(jnp.float32)
            delta = jnp.sum(g_i.astype(jnp.float32).T * out, axis=0, keepdims=True)
            b_o[rows, :] = out.T
            grad_p = matmul(v_s[keys, :], g_i, 1, 1)
            grad_s = (probs * (grad_p - delta)).astype(jnp.bfloat16)
            b_v[keys, :] += matmul(probs_low, g_i, 1, 0)
            b_k[keys, :] += matmul(grad_s, q_i, 1, 0)
            b_q[rows, :] = (matmul(kt_s[n], grad_s, 1, 0) * factor).T
            return carry

        lax.fori_loop(0, HALF // BLK, query_block, 0)

    for buf in (b_q, b_k, b_v, b_o):
        repeat(buf)
    for z in range(ZN):
        for n, side in enumerate(out_sides):
            ref, at = (grads_out[0], n) if len(grads_out) == 1 else (grads_out[n], 0)
            rows = pl.ds(wrap(side * HALF + z * TILE - shift), TILE)
            ref[z, at, :TILE, :] = b_q[rows, :].astype(jnp.bfloat16)
            ref[z, at, TILE : 2 * TILE, :] = (b_k[rows, :] * factor).astype(jnp.bfloat16)
            ref[z, at, 2 * TILE :, :] = b_v[rows, :].astype(jnp.bfloat16)
        for c in range(2):
            rows = pl.ds(wrap(c * HALF + z * TILE - shift), TILE)
            o_out[z, c] = b_o[rows, :].astype(jnp.bfloat16)


def attend(info, one, two, grad_attn, chunk):
    flat = (SEQ, HD)
    whole, half = (ZN, 2, 3 * TILE, HD), (ZN, 1, 3 * TILE, HD)
    first = pl.BlockSpec(half, lambda i, info: (0, 0, 0, 0))
    in_specs = [first, pl.BlockSpec(half, lambda i, info: (0, 1, 0, 0))]
    if chunk == 0:
        out_specs = [pl.BlockSpec(whole, lambda i, info: (0, 0, 0, 0))]
        shapes = [whole]
    else:
        out_specs = [pl.BlockSpec(half, lambda i, info: (0, info[0], 0, 0)), first]
        shapes = [whole, half]
    return pl.pallas_call(
        attend_kernel,
        grid_spec=pltpu.PrefetchScalarGridSpec(
            num_scalar_prefetch=1,
            grid=(1,),
            in_specs=in_specs
            + [pl.BlockSpec((ZN, 2, TILE, HD), lambda i, info: (0, 0, 0, chunk))],
            out_specs=out_specs + [pl.BlockSpec((ZN, 2, TILE, HD), lambda i, info: (0, 0, 0, 0))],
            scratch_shapes=[pltpu.VMEM(flat, jnp.bfloat16)] * 4
            + [pltpu.VMEM((2, HD, HALF), jnp.bfloat16)] * 2
            + [pltpu.VMEM((SEQ + TILE, HD), jnp.float32)] * 4,
        ),
        out_shape=[jax.ShapeDtypeStruct(s, jnp.bfloat16) for s in shapes + [(ZN, 2, TILE, HD)]],
        compiler_params=params(),
        cost_estimate=pl.CostEstimate(
            flops=24 * SEQ * SEQ * HD, bytes_accessed=8 << 20, transcendentals=SEQ * SEQ // 2
        ),
        name=f"attend{chunk}",
    )(info, one, two, grad_attn)


def project_kernel(rows_ref, weight_ref, out_ref):
    out = matmul(rows_ref[...], weight_ref[...], 1, 1).astype(jnp.bfloat16)
    for n in range(out.shape[0] // TILE):
        out_ref[n // 2, n % 2] = out[n * TILE : (n + 1) * TILE]


def project(rows, weights):
    width = rows.shape[1]
    return pl.pallas_call(
        project_kernel,
        grid=(SEQ // BLK,),
        in_specs=[
            pl.BlockSpec((BLK, width), lambda i: (i, 0)),
            pl.BlockSpec((2 * HD, width), lambda i: (0, 0)),
        ],
        out_specs=pl.BlockSpec((BLK // TILE // 2, 2, TILE, 2 * HD), lambda i: (i, 0, 0, 0)),
        out_shape=jax.ShapeDtypeStruct((ZN, 2, TILE, 2 * HD), jnp.bfloat16),
        compiler_params=params(),
        cost_estimate=pl.CostEstimate(
            flops=4 * SEQ * HD * width, bytes_accessed=10 << 20, transcendentals=0
        ),
        name="project",
    )(rows, weights)


def exchange(blocks):
    flat = blocks.reshape(2 * ZN, 3 * TILE, HD)
    moved = lax.all_to_all(flat, ("z", "c"), split_axis=0, concat_axis=0, tiled=True)
    return moved.reshape(blocks.shape)


def weight_term(out, rows):
    return jnp.einsum(
        "tf,tc->fc", out.reshape(SEQ, HD), rows, preferred_element_type=jnp.float32
    )


def sum_planes(term):
    y = lax.axis_index("y")
    low, high = lax.bitwise_and(y, 1) == 0, y < 2
    parts = [term[:, i * 512 : (i + 1) * 512] for i in range(4)]
    even = jnp.concatenate([parts[0], parts[2]], axis=1)
    odd = jnp.concatenate([parts[1], parts[3]], axis=1)
    send = jnp.where(low, odd, even).astype(jnp.bfloat16)
    got = lax.ppermute(send, "y", [(0, 1), (1, 0), (2, 3), (3, 2)])
    both = jnp.where(low, even, odd) + got.astype(jnp.float32)
    send = jnp.where(high, both[:, 512:], both[:, :512]).astype(jnp.bfloat16)
    got = lax.ppermute(send, "y", [(0, 2), (2, 0), (1, 3), (3, 1)])
    return jnp.where(high, both[:, :512], both[:, 512:]) + got.astype(jnp.float32)


def swap(array):
    return lax.ppermute(array, ("xh", "c"), TRANSPOSE)


def on_device(queries, key_rows, values, upstream, out_weight, doc_lengths):
    xs, xh = lax.axis_index("xs"), lax.axis_index("xh")
    group_rows = swap(upstream[0])
    tok_rows = lax.all_gather(group_rows, ("z", "c"), axis=0, tiled=True)

    first = pack(queries, key_rows, values, 0)
    first, group_rows = lax.optimization_barrier((first, group_rows))
    first = swap(first)

    weight = lax.all_gather(out_weight, ("y", "c"), axis=1, tiled=True)
    first, weight = lax.optimization_barrier((first, weight))
    first = exchange(first)

    second = swap(pack(queries, key_rows, values, 1))
    second, weight = lax.optimization_barrier((second, weight))
    weight = lax.ppermute(weight, ("xs", "c"), TRANSPOSE)
    other_weight = lax.ppermute(weight, "xh", SWAP)
    weights = jnp.concatenate(
        [jnp.where(xh == 0, weight, other_weight), jnp.where(xh == 0, other_weight, weight)]
    )
    lengths = lax.dynamic_index_in_dim(doc_lengths[0], xs, 0, keepdims=False)
    lengths = swap(lengths)
    ends = jnp.cumsum(lengths)
    shift = jnp.sum(jnp.where(lengths == HALF, ends - HALF, 0), dtype=jnp.int32)
    info = jnp.concatenate([jnp.stack([xh.astype(jnp.int32), shift]), ends])
    second, first, weights, info = lax.optimization_barrier((second, first, weights, info))
    second = exchange(second)

    grad_attn = project(tok_rows, weights)
    grads, out = attend(info, first, first, grad_attn, 0)
    term = weight_term(out, tok_rows)
    grads, second, term = lax.optimization_barrier((grads, second, term))
    sums = [sum_planes(term)]
    grads = exchange(grads)
    near, far, out = attend(info, second, second, grad_attn, 1)
    back = put_other(info, lax.ppermute(far, "xh", SWAP), near)
    term = weight_term(out, tok_rows)
    back, grads, term, sums = lax.optimization_barrier((back, grads, term, sums))
    back = exchange(back)
    grads = swap(grads)
    grads, sums = lax.optimization_barrier((grads, [*sums, sum_planes(term)]))

    send = jnp.where(xh == 0, sums[1], sums[0]).astype(jnp.bfloat16)
    total = jnp.where(xh == 0, sums[0], sums[1]) + lax.ppermute(send, "xh", SWAP).astype(jnp.float32)
    one, two = total[:, :256], total[:, 256:]
    straight = lax.ppermute(jnp.where(xs == 0, one, two), ("xs", "c"), TRANSPOSE)
    crossed = lax.ppermute(
        jnp.where(xs == 0, two, one), ("xs", "c"), [(0, 1), (1, 3), (2, 0), (3, 2)]
    )
    grad_weight = straight + crossed
    held = unpack(grads, 0, ())
    held = unpack(back, 1, held)
    return (*held, grad_weight)


def solution(mesh):
    fine = Mesh(mesh.devices.reshape(2, 2, ZN, 4, 2), ("xs", "xh", "z", "y", "c"))
    ctx, dp = ("xs", "xh", "z"), ("y", "c")
    rows = P(dp, ctx, None)
    return jax.shard_map(
        on_device,
        mesh=fine,
        in_specs=(rows, rows, rows, rows, P(ctx, dp), P(dp, None, None)),
        out_specs=(rows, rows, rows, P(ctx, dp)),
        check_vma=False,
    )
```

```python
import functools

import jax
import jax.numpy as jnp
from jax import lax
from jax.experimental import pallas as pl
from jax.experimental.pallas import tpu as pltpu
from jax.sharding import Mesh, PartitionSpec as P

HD = 128
SEQS = 2
ZN = 8
TILE = 128
SEQ = 2048
HALF = SEQ // 2
BLK = 512
SWAP = [(0, 1), (1, 0)]
TRANSPOSE = [(0, 0), (1, 2), (2, 1), (3, 3)]
LOW = -1e30
VMEM_LIMIT = 48 * 1024 * 1024


def params():
    return pltpu.CompilerParams(vmem_limit_bytes=VMEM_LIMIT)


def matmul(lhs, rhs, left, right):
    return lax.dot_general(
        lhs, rhs, (((left,), (right,)), ((), ())), preferred_element_type=jnp.float32
    )


def pack_kernel(chunk, q_ref, k_ref, v_ref, out_ref, sems):
    copies = []
    for c in range(2):
        for z in range(ZN):
            for t, ref in enumerate((q_ref, k_ref, v_ref)):
                col = ((2 * c + chunk) * ZN + z) * HD
                copies.append(
                    pltpu.make_async_copy(
                        ref.at[0, :, pl.ds(col, HD)],
                        out_ref.at[z, c, pl.ds(t * TILE, TILE), :],
                        sems.at[len(copies)],
                    )
                )
                copies[-1].start()
    for copy in copies:
        copy.wait()


def pack(queries, keys, values, chunk):
    return pl.pallas_call(
        functools.partial(pack_kernel, chunk),
        in_specs=[pl.BlockSpec(memory_space=pltpu.HBM)] * 3,
        out_specs=pl.BlockSpec(memory_space=pltpu.HBM),
        out_shape=jax.ShapeDtypeStruct((ZN, 2, 3 * TILE, HD), jnp.bfloat16),
        scratch_shapes=[pltpu.SemaphoreType.DMA((6 * ZN,))],
        compiler_params=params(),
        name=f"pack{chunk}",
    )(queries, keys, values)


def unpack_kernel(in_ref, *refs):
    for z in range(ZN):
        for t, ref in enumerate(refs[-3:]):
            ref[0, :, z * HD : (z + 1) * HD] = in_ref[z, 0, t * TILE : (t + 1) * TILE, :]


def unpack(blocks, chunk, held):
    rows = pl.BlockSpec((1, TILE, ZN * HD), lambda c: (0, 0, 2 * c + chunk))
    whole = jax.ShapeDtypeStruct((1, TILE, 4 * ZN * HD), jnp.bfloat16)
    return pl.pallas_call(
        unpack_kernel,
        grid=(2,),
        in_specs=[pl.BlockSpec((ZN, 1, 3 * TILE, HD), lambda c: (0, c, 0, 0))]
        + [pl.BlockSpec(memory_space=pl.ANY)] * len(held),
        out_specs=[rows] * 3,
        out_shape=[whole] * 3,
        input_output_aliases={i + 1: i for i in range(len(held))},
        compiler_params=params(),
        name=f"unpack{chunk}",
    )(blocks, *held)


def take_kernel(info_ref, in_ref, out_ref):
    out_ref[...] = in_ref[...]


def take_other(info, blocks):
    half = (ZN, 1, 3 * TILE, HD)
    return pl.pallas_call(
        take_kernel,
        grid_spec=pltpu.PrefetchScalarGridSpec(
            num_scalar_prefetch=1,
            grid=(1,),
            in_specs=[pl.BlockSpec(half, lambda i, info: (0, 1 - info[0], 0, 0))],
            out_specs=pl.BlockSpec(half, lambda i, info: (0, 0, 0, 0)),
        ),
        out_shape=jax.ShapeDtypeStruct(half, jnp.bfloat16),
        compiler_params=params(),
        name="take",
    )(info, blocks)


def put_kernel(info_ref, in_ref, held_ref, out_ref):
    out_ref[...] = in_ref[...]


def put_other(info, part, blocks):
    return pl.pallas_call(
        put_kernel,
        grid_spec=pltpu.PrefetchScalarGridSpec(
            num_scalar_prefetch=1,
            grid=(1,),
            in_specs=[
                pl.BlockSpec((ZN, 1, 3 * TILE, HD), lambda i, info: (0, 0, 0, 0)),
                pl.BlockSpec(memory_space=pl.ANY),
            ],
            out_specs=pl.BlockSpec((ZN, 1, 3 * TILE, HD), lambda i, info: (0, 1 - info[0], 0, 0)),
        ),
        out_shape=jax.ShapeDtypeStruct((ZN, 2, 3 * TILE, HD), jnp.bfloat16),
        input_output_aliases={2: 0},
        compiler_params=params(),
        name="put",
    )(info, part, blocks)


def attend_kernel(info, one, two, g, *refs):
    *grads_out, o_out, q_s, k_s, v_s, g_s, kt_s, vt_s, b_q, b_k, b_v, b_o = refs
    factor = HD ** (-0.5)
    shift = info[1]
    tiles = SEQ // TILE
    sides = (info[0], 1 - info[0])
    in_sides, out_sides = (sides, (0, 1)) if len(grads_out) == 1 else ((0, 1), sides)

    def wrap(row):
        return jnp.where(row < 0, row + SEQ, jnp.where(row >= SEQ, row - SEQ, row))

    def repeat(buf):
        buf[SEQ:, :] = buf[:TILE, :]

    for side, part in zip(in_sides, (one, two)):
        for z in range(ZN):
            rows = pl.ds(pl.multiple_of(side * HALF + z * TILE, TILE), TILE)
            for t, buf in enumerate((b_q, b_k, b_v)):
                buf[rows, :] = part[z, 0, t * TILE : (t + 1) * TILE, :].astype(jnp.float32)
    for z in range(ZN):
        for c in range(2):
            row = c * HALF + z * TILE
            b_o[row : row + TILE, :] = g[z, c].astype(jnp.float32)
    for buf, ref in ((b_q, q_s), (b_k, k_s), (b_v, v_s), (b_o, g_s)):
        repeat(buf)
        for j in range(tiles):
            rows = pl.ds(wrap(shift + j * TILE), TILE)
            ref[j * TILE : (j + 1) * TILE, :] = buf[rows, :].astype(jnp.bfloat16)
    for n in range(2):
        kt_s[n] = k_s[n * HALF : (n + 1) * HALF, :].T
        vt_s[n] = v_s[n * HALF : (n + 1) * HALF, :].T
    b_k[...] = jnp.zeros_like(b_k)
    b_v[...] = jnp.zeros_like(b_v)
    ends = [wrap(info[2 + d] - shift) for d in range(8)]

    for n in range(2):
        low = n * HALF
        keys = slice(low, low + HALF)

        def query_block(i, carry):
            rows = pl.ds(pl.multiple_of(low + i * BLK, BLK), BLK)
            q_i, g_i = q_s[rows, :], g_s[rows, :]
            s = matmul(k_s[keys, :], q_i, 1, 1)
            if n == 1:
                place = low + i * BLK + lax.broadcasted_iota(jnp.int32, (1, BLK), 1)
                start, stop = jnp.full_like(place, HALF), jnp.full_like(place, SEQ)
                for end in ends:
                    start = jnp.maximum(start, jnp.where(end <= place, end, HALF))
                    stop = jnp.minimum(stop, jnp.where(end > place, end, SEQ))
                seen = low + lax.broadcasted_iota(jnp.int32, (HALF, BLK), 0)
                s = jnp.where((seen >= start) & (seen < stop), s, LOW)
            top = jnp.max(s, axis=0, keepdims=True)
            probs = jnp.exp((s - top) * factor)
            probs = probs * (1.0 / jnp.sum(probs, axis=0, keepdims=True))
            probs_low = probs.astype(jnp.bfloat16)
            out = matmul(vt_s[n], probs_low, 1, 0).astype(jnp.bfloat16).astype(jnp.float32)
            delta = jnp.sum(g_i.astype(jnp.float32).T * out, axis=0, keepdims=True)
            b_o[rows, :] = out.T
            grad_p = matmul(v_s[keys, :], g_i, 1, 1)
            grad_s = (probs * (grad_p - delta)).astype(jnp.bfloat16)
            b_v[keys, :] += matmul(probs_low, g_i, 1, 0)
            b_k[keys, :] += matmul(grad_s, q_i, 1, 0)
            b_q[rows, :] = (matmul(kt_s[n], grad_s, 1, 0) * factor).T
            return carry

        lax.fori_loop(0, HALF // BLK, query_block, 0)

    for buf in (b_q, b_k, b_v, b_o):
        repeat(buf)
    for z in range(ZN):
        for n, side in enumerate(out_sides):
            ref, at = (grads_out[0], n) if len(grads_out) == 1 else (grads_out[n], 0)
            rows = pl.ds(wrap(side * HALF + z * TILE - shift), TILE)
            ref[z, at, :TILE, :] = b_q[rows, :].astype(jnp.bfloat16)
            ref[z, at, TILE : 2 * TILE, :] = (b_k[rows, :] * factor).astype(jnp.bfloat16)
            ref[z, at, 2 * TILE :, :] = b_v[rows, :].astype(jnp.bfloat16)
        for c in range(2):
            rows = pl.ds(wrap(c * HALF + z * TILE - shift), TILE)
            o_out[z, c] = b_o[rows, :].astype(jnp.bfloat16)


def attend(info, one, two, grad_attn, chunk):
    flat = (SEQ, HD)
    whole, half = (ZN, 2, 3 * TILE, HD), (ZN, 1, 3 * TILE, HD)
    first = pl.BlockSpec(half, lambda i, info: (0, 0, 0, 0))
    if chunk == 0:
        in_specs = [pl.BlockSpec(half, lambda i, info: (0, info[0], 0, 0)), first]
        out_specs = [pl.BlockSpec(whole, lambda i, info: (0, 0, 0, 0))]
        shapes = [whole]
    else:
        in_specs = [first, pl.BlockSpec(half, lambda i, info: (0, 1, 0, 0))]
        out_specs = [pl.BlockSpec(half, lambda i, info: (0, info[0], 0, 0)), first]
        shapes = [whole, half]
    return pl.pallas_call(
        attend_kernel,
        grid_spec=pltpu.PrefetchScalarGridSpec(
            num_scalar_prefetch=1,
            grid=(1,),
            in_specs=in_specs
            + [pl.BlockSpec((ZN, 2, TILE, HD), lambda i, info: (0, 0, 0, chunk))],
            out_specs=out_specs + [pl.BlockSpec((ZN, 2, TILE, HD), lambda i, info: (0, 0, 0, 0))],
            scratch_shapes=[pltpu.VMEM(flat, jnp.bfloat16)] * 4
            + [pltpu.VMEM((2, HD, HALF), jnp.bfloat16)] * 2
            + [pltpu.VMEM((SEQ + TILE, HD), jnp.float32)] * 4,
        ),
        out_shape=[jax.ShapeDtypeStruct(s, jnp.bfloat16) for s in shapes + [(ZN, 2, TILE, HD)]],
        compiler_params=params(),
        cost_estimate=pl.CostEstimate(
            flops=24 * SEQ * SEQ * HD, bytes_accessed=8 << 20, transcendentals=SEQ * SEQ // 2
        ),
        name=f"attend{chunk}",
    )(info, one, two, grad_attn)


def project_kernel(rows_ref, weight_ref, out_ref):
    out = matmul(rows_ref[...], weight_ref[...], 1, 1).astype(jnp.bfloat16)
    for n in range(out.shape[0] // TILE):
        out_ref[n // 2, n % 2] = out[n * TILE : (n + 1) * TILE]


def project(rows, weights):
    width = rows.shape[1]
    return pl.pallas_call(
        project_kernel,
        grid=(SEQ // BLK,),
        in_specs=[
            pl.BlockSpec((BLK, width), lambda i: (i, 0)),
            pl.BlockSpec((2 * HD, width), lambda i: (0, 0)),
        ],
        out_specs=pl.BlockSpec((BLK // TILE // 2, 2, TILE, 2 * HD), lambda i: (i, 0, 0, 0)),
        out_shape=jax.ShapeDtypeStruct((ZN, 2, TILE, 2 * HD), jnp.bfloat16),
        compiler_params=params(),
        cost_estimate=pl.CostEstimate(
            flops=4 * SEQ * HD * width, bytes_accessed=10 << 20, transcendentals=0
        ),
        name="project",
    )(rows, weights)


def exchange(blocks):
    flat = blocks.reshape(2 * ZN, 3 * TILE, HD)
    moved = lax.all_to_all(flat, ("z", "c"), split_axis=0, concat_axis=0, tiled=True)
    return moved.reshape(blocks.shape)


def weight_term(out, rows):
    return jnp.einsum(
        "tf,tc->fc", out.reshape(SEQ, HD), rows, preferred_element_type=jnp.float32
    )


def sum_planes(term):
    y = lax.axis_index("y")
    low, high = lax.bitwise_and(y, 1) == 0, y < 2
    parts = [term[:, i * 512 : (i + 1) * 512] for i in range(4)]
    even = jnp.concatenate([parts[0], parts[2]], axis=1)
    odd = jnp.concatenate([parts[1], parts[3]], axis=1)
    send = jnp.where(low, odd, even).astype(jnp.bfloat16)
    got = lax.ppermute(send, "y", [(0, 1), (1, 0), (2, 3), (3, 2)])
    both = jnp.where(low, even, odd) + got.astype(jnp.float32)
    send = jnp.where(high, both[:, 512:], both[:, :512]).astype(jnp.bfloat16)
    got = lax.ppermute(send, "y", [(0, 2), (2, 0), (1, 3), (3, 1)])
    return jnp.where(high, both[:, :512], both[:, 512:]) + got.astype(jnp.float32)


def swap(array):
    return lax.ppermute(array, ("xh", "c"), TRANSPOSE)


def on_device(queries, key_rows, values, upstream, out_weight, doc_lengths):
    xs, xh = lax.axis_index("xs"), lax.axis_index("xh")
    first = exchange(pack(queries, key_rows, values, 0))
    group_rows = swap(upstream[0])
    tok_rows = lax.all_gather(group_rows, ("z", "c"), axis=0, tiled=True)

    second = pack(queries, key_rows, values, 1)
    second, out_weight, group_rows = lax.optimization_barrier((second, out_weight, group_rows))
    second = swap(second)
    weight = lax.all_gather(out_weight, ("y", "c"), axis=1, tiled=True)
    second, weight = lax.optimization_barrier((second, weight))
    weight = lax.ppermute(weight, ("xs", "c"), TRANSPOSE)
    lengths = lax.dynamic_index_in_dim(doc_lengths[0], xs, 0, keepdims=False)
    lengths = swap(lengths)
    ends = jnp.cumsum(lengths)
    shift = jnp.sum(jnp.where(lengths == HALF, ends - HALF, 0), dtype=jnp.int32)
    info = jnp.concatenate([jnp.stack([xh.astype(jnp.int32), shift]), ends])
    first, weight, info = lax.optimization_barrier((first, weight, info))
    other_weight = lax.ppermute(weight, "xh", SWAP)
    second, first, other_weight = lax.optimization_barrier((second, first, other_weight))
    other = lax.ppermute(take_other(info, first), "xh", SWAP)
    second = exchange(second)

    weights = jnp.concatenate(
        [jnp.where(xh == 0, weight, other_weight), jnp.where(xh == 0, other_weight, weight)]
    )
    grad_attn = project(tok_rows, weights)
    grads, out = attend(info, first, other, grad_attn, 0)
    term = weight_term(out, tok_rows)
    grads, second, term = lax.optimization_barrier((grads, second, term))
    sums = [sum_planes(term)]
    grads = exchange(grads)
    near, far, out = attend(info, second, second, grad_attn, 1)
    back = put_other(info, lax.ppermute(far, "xh", SWAP), near)
    term = weight_term(out, tok_rows)
    back, grads, term, sums = lax.optimization_barrier((back, grads, term, sums))
    back = exchange(back)
    grads = swap(grads)
    grads, sums = lax.optimization_barrier((grads, [*sums, sum_planes(term)]))

    send = jnp.where(xh == 0, sums[1], sums[0]).astype(jnp.bfloat16)
    total = jnp.where(xh == 0, sums[0], sums[1]) + lax.ppermute(send, "xh", SWAP).astype(jnp.float32)
    one, two = total[:, :256], total[:, 256:]
    straight = lax.ppermute(jnp.where(xs == 0, one, two), ("xs", "c"), TRANSPOSE)
    crossed = lax.ppermute(
        jnp.where(xs == 0, two, one), ("xs", "c"), [(0, 1), (1, 3), (2, 0), (3, 2)]
    )
    grad_weight = straight + crossed
    held = unpack(grads, 0, ())
    held = unpack(back, 1, held)
    return (*held, grad_weight)


def solution(mesh):
    fine = Mesh(mesh.devices.reshape(2, 2, ZN, 4, 2), ("xs", "xh", "z", "y", "c"))
    ctx, dp = ("xs", "xh", "z"), ("y", "c")
    rows = P(dp, ctx, None)
    return jax.shard_map(
        on_device,
        mesh=fine,
        in_specs=(rows, rows, rows, rows, P(ctx, dp), P(dp, None, None)),
        out_specs=(rows, rows, rows, P(ctx, dp)),
        check_vma=False,
    )
```

```python
import jax
import jax.numpy as jnp
from jax import lax
from jax.experimental import pallas as pl
from jax.experimental.pallas import tpu as pltpu
from jax.sharding import Mesh, PartitionSpec as P

HD = 128
SEQS = 2
ZN = 8
TILE = 128
SEQ = 2048
HALF = SEQ // 2
BLK = 512
SWAP = [(0, 1), (1, 0)]
TRANSPOSE = [(0, 0), (1, 2), (2, 1), (3, 3)]
LOW = -1e30
VMEM_LIMIT = 48 * 1024 * 1024


def params(limit=VMEM_LIMIT):
    return pltpu.CompilerParams(vmem_limit_bytes=limit)


def matmul(lhs, rhs, left, right):
    return lax.dot_general(
        lhs, rhs, (((left,), (right,)), ((), ())), preferred_element_type=jnp.float32
    )


def pack_kernel(q_ref, k_ref, v_ref, out_ref):
    for z in range(ZN):
        for t, ref in enumerate((q_ref, k_ref, v_ref)):
            out_ref[z, 0, t * TILE : (t + 1) * TILE, :] = ref[0, :, z * HD : (z + 1) * HD]


def pack(queries, keys, values, chunk):
    rows = pl.BlockSpec((1, TILE, ZN * HD), lambda c: (0, 0, 2 * c + chunk))
    return pl.pallas_call(
        pack_kernel,
        grid=(2,),
        in_specs=[rows] * 3,
        out_specs=pl.BlockSpec((ZN, 1, 3 * TILE, HD), lambda c: (0, c, 0, 0)),
        out_shape=jax.ShapeDtypeStruct((ZN, 2, 3 * TILE, HD), jnp.bfloat16),
        compiler_params=params(60 * 1024 * 1024),
        name=f"pack{chunk}",
    )(queries, keys, values)


def unpack_kernel(in_ref, *refs):
    for z in range(ZN):
        for t, ref in enumerate(refs[-3:]):
            ref[0, :, z * HD : (z + 1) * HD] = in_ref[z, 0, t * TILE : (t + 1) * TILE, :]


def unpack(blocks, chunk, held):
    rows = pl.BlockSpec((1, TILE, ZN * HD), lambda c: (0, 0, 2 * c + chunk))
    whole = jax.ShapeDtypeStruct((1, TILE, 4 * ZN * HD), jnp.bfloat16)
    return pl.pallas_call(
        unpack_kernel,
        grid=(2,),
        in_specs=[pl.BlockSpec((ZN, 1, 3 * TILE, HD), lambda c: (0, c, 0, 0))]
        + [pl.BlockSpec(memory_space=pl.ANY)] * len(held),
        out_specs=[rows] * 3,
        out_shape=[whole] * 3,
        input_output_aliases={i + 1: i for i in range(len(held))},
        compiler_params=params(),
        name=f"unpack{chunk}",
    )(blocks, *held)


def take_kernel(info_ref, in_ref, out_ref):
    out_ref[...] = in_ref[...]


def take_other(info, blocks):
    half = (ZN, 1, 3 * TILE, HD)
    return pl.pallas_call(
        take_kernel,
        grid_spec=pltpu.PrefetchScalarGridSpec(
            num_scalar_prefetch=1,
            grid=(1,),
            in_specs=[pl.BlockSpec(half, lambda i, info: (0, 1 - info[0], 0, 0))],
            out_specs=pl.BlockSpec(half, lambda i, info: (0, 0, 0, 0)),
        ),
        out_shape=jax.ShapeDtypeStruct(half, jnp.bfloat16),
        compiler_params=params(),
        name="take",
    )(info, blocks)


def put_kernel(info_ref, in_ref, held_ref, out_ref):
    out_ref[...] = in_ref[...]


def put_other(info, part, blocks):
    return pl.pallas_call(
        put_kernel,
        grid_spec=pltpu.PrefetchScalarGridSpec(
            num_scalar_prefetch=1,
            grid=(1,),
            in_specs=[
                pl.BlockSpec((ZN, 1, 3 * TILE, HD), lambda i, info: (0, 0, 0, 0)),
                pl.BlockSpec(memory_space=pl.ANY),
            ],
            out_specs=pl.BlockSpec((ZN, 1, 3 * TILE, HD), lambda i, info: (0, 1 - info[0], 0, 0)),
        ),
        out_shape=jax.ShapeDtypeStruct((ZN, 2, 3 * TILE, HD), jnp.bfloat16),
        input_output_aliases={2: 0},
        compiler_params=params(),
        name="put",
    )(info, part, blocks)


def attend_kernel(info, one, two, g, *refs):
    *grads_out, o_out, q_s, k_s, v_s, g_s, kt_s, vt_s, b_q, b_k, b_v, b_o = refs
    factor = HD ** (-0.5)
    shift = info[1]
    tiles = SEQ // TILE
    sides = (info[0], 1 - info[0])
    in_sides, out_sides = (sides, (0, 1)) if len(grads_out) == 1 else ((0, 1), sides)

    def wrap(row):
        return jnp.where(row < 0, row + SEQ, jnp.where(row >= SEQ, row - SEQ, row))

    def repeat(buf):
        buf[SEQ:, :] = buf[:TILE, :]

    for side, part in zip(in_sides, (one, two)):
        for z in range(ZN):
            rows = pl.ds(pl.multiple_of(side * HALF + z * TILE, TILE), TILE)
            for t, buf in enumerate((b_q, b_k, b_v)):
                buf[rows, :] = part[z, 0, t * TILE : (t + 1) * TILE, :].astype(jnp.float32)
    for z in range(ZN):
        for c in range(2):
            row = c * HALF + z * TILE
            b_o[row : row + TILE, :] = g[z, c].astype(jnp.float32)
    for buf, ref in ((b_q, q_s), (b_k, k_s), (b_v, v_s), (b_o, g_s)):
        repeat(buf)
        for j in range(tiles):
            rows = pl.ds(wrap(shift + j * TILE), TILE)
            ref[j * TILE : (j + 1) * TILE, :] = buf[rows, :].astype(jnp.bfloat16)
    for n in range(2):
        kt_s[n] = k_s[n * HALF : (n + 1) * HALF, :].T
        vt_s[n] = v_s[n * HALF : (n + 1) * HALF, :].T
    b_k[...] = jnp.zeros_like(b_k)
    b_v[...] = jnp.zeros_like(b_v)
    ends = [wrap(info[2 + d] - shift) for d in range(8)]

    for n in range(2):
        low = n * HALF
        keys = slice(low, low + HALF)

        def query_block(i, carry):
            rows = pl.ds(pl.multiple_of(low + i * BLK, BLK), BLK)
            q_i, g_i = q_s[rows, :], g_s[rows, :]
            s = matmul(k_s[keys, :], q_i, 1, 1)
            if n == 1:
                place = low + i * BLK + lax.broadcasted_iota(jnp.int32, (1, BLK), 1)
                start, stop = jnp.full_like(place, HALF), jnp.full_like(place, SEQ)
                for end in ends:
                    start = jnp.maximum(start, jnp.where(end <= place, end, HALF))
                    stop = jnp.minimum(stop, jnp.where(end > place, end, SEQ))
                seen = low + lax.broadcasted_iota(jnp.int32, (HALF, BLK), 0)
                s = jnp.where((seen >= start) & (seen < stop), s, LOW)
            top = jnp.max(s, axis=0, keepdims=True)
            probs = jnp.exp((s - top) * factor)
            probs = probs * (1.0 / jnp.sum(probs, axis=0, keepdims=True))
            probs_low = probs.astype(jnp.bfloat16)
            out = matmul(vt_s[n], probs_low, 1, 0).astype(jnp.bfloat16).astype(jnp.float32)
            delta = jnp.sum(g_i.astype(jnp.float32).T * out, axis=0, keepdims=True)
            b_o[rows, :] = out.T
            grad_p = matmul(v_s[keys, :], g_i, 1, 1)
            grad_s = (probs * (grad_p - delta)).astype(jnp.bfloat16)
            b_v[keys, :] += matmul(probs_low, g_i, 1, 0)
            b_k[keys, :] += matmul(grad_s, q_i, 1, 0)
            b_q[rows, :] = (matmul(kt_s[n], grad_s, 1, 0) * factor).T
            return carry

        lax.fori_loop(0, HALF // BLK, query_block, 0)

    for buf in (b_q, b_k, b_v, b_o):
        repeat(buf)
    for z in range(ZN):
        for n, side in enumerate(out_sides):
            ref, at = (grads_out[0], n) if len(grads_out) == 1 else (grads_out[n], 0)
            rows = pl.ds(wrap(side * HALF + z * TILE - shift), TILE)
            ref[z, at, :TILE, :] = b_q[rows, :].astype(jnp.bfloat16)
            ref[z, at, TILE : 2 * TILE, :] = (b_k[rows, :] * factor).astype(jnp.bfloat16)
            ref[z, at, 2 * TILE :, :] = b_v[rows, :].astype(jnp.bfloat16)
        for c in range(2):
            rows = pl.ds(wrap(c * HALF + z * TILE - shift), TILE)
            o_out[z, c] = b_o[rows, :].astype(jnp.bfloat16)


def attend(info, one, two, grad_attn, chunk):
    flat = (SEQ, HD)
    whole, half = (ZN, 2, 3 * TILE, HD), (ZN, 1, 3 * TILE, HD)
    first = pl.BlockSpec(half, lambda i, info: (0, 0, 0, 0))
    if chunk == 0:
        in_specs = [pl.BlockSpec(half, lambda i, info: (0, info[0], 0, 0)), first]
        out_specs = [pl.BlockSpec(whole, lambda i, info: (0, 0, 0, 0))]
        shapes = [whole]
    else:
        in_specs = [first, pl.BlockSpec(half, lambda i, info: (0, 1, 0, 0))]
        out_specs = [pl.BlockSpec(half, lambda i, info: (0, info[0], 0, 0)), first]
        shapes = [whole, half]
    return pl.pallas_call(
        attend_kernel,
        grid_spec=pltpu.PrefetchScalarGridSpec(
            num_scalar_prefetch=1,
            grid=(1,),
            in_specs=in_specs
            + [pl.BlockSpec((ZN, 2, TILE, HD), lambda i, info: (0, 0, 0, chunk))],
            out_specs=out_specs + [pl.BlockSpec((ZN, 2, TILE, HD), lambda i, info: (0, 0, 0, 0))],
            scratch_shapes=[pltpu.VMEM(flat, jnp.bfloat16)] * 4
            + [pltpu.VMEM((2, HD, HALF), jnp.bfloat16)] * 2
            + [pltpu.VMEM((SEQ + TILE, HD), jnp.float32)] * 4,
        ),
        out_shape=[jax.ShapeDtypeStruct(s, jnp.bfloat16) for s in shapes + [(ZN, 2, TILE, HD)]],
        compiler_params=params(),
        cost_estimate=pl.CostEstimate(
            flops=24 * SEQ * SEQ * HD, bytes_accessed=8 << 20, transcendentals=SEQ * SEQ // 2
        ),
        name=f"attend{chunk}",
    )(info, one, two, grad_attn)


def project_kernel(rows_ref, weight_ref, out_ref):
    out = matmul(rows_ref[...], weight_ref[...], 1, 1).astype(jnp.bfloat16)
    for n in range(out.shape[0] // TILE):
        out_ref[n // 2, n % 2] = out[n * TILE : (n + 1) * TILE]


def project(rows, weights):
    width = rows.shape[1]
    return pl.pallas_call(
        project_kernel,
        grid=(SEQ // BLK,),
        in_specs=[
            pl.BlockSpec((BLK, width), lambda i: (i, 0)),
            pl.BlockSpec((2 * HD, width), lambda i: (0, 0)),
        ],
        out_specs=pl.BlockSpec((BLK // TILE // 2, 2, TILE, 2 * HD), lambda i: (i, 0, 0, 0)),
        out_shape=jax.ShapeDtypeStruct((ZN, 2, TILE, 2 * HD), jnp.bfloat16),
        compiler_params=params(),
        cost_estimate=pl.CostEstimate(
            flops=4 * SEQ * HD * width, bytes_accessed=10 << 20, transcendentals=0
        ),
        name="project",
    )(rows, weights)


def exchange(blocks):
    flat = blocks.reshape(2 * ZN, 3 * TILE, HD)
    moved = lax.all_to_all(flat, ("z", "c"), split_axis=0, concat_axis=0, tiled=True)
    return moved.reshape(blocks.shape)


def weight_term(out, rows):
    return jnp.einsum(
        "tf,tc->fc", out.reshape(SEQ, HD), rows, preferred_element_type=jnp.float32
    )


def sum_planes(term):
    y = lax.axis_index("y")
    low, high = lax.bitwise_and(y, 1) == 0, y < 2
    parts = [term[:, i * 512 : (i + 1) * 512] for i in range(4)]
    even = jnp.concatenate([parts[0], parts[2]], axis=1)
    odd = jnp.concatenate([parts[1], parts[3]], axis=1)
    send = jnp.where(low, odd, even).astype(jnp.bfloat16)
    got = lax.ppermute(send, "y", [(0, 1), (1, 0), (2, 3), (3, 2)])
    both = jnp.where(low, even, odd) + got.astype(jnp.float32)
    send = jnp.where(high, both[:, 512:], both[:, :512]).astype(jnp.bfloat16)
    got = lax.ppermute(send, "y", [(0, 2), (2, 0), (1, 3), (3, 1)])
    return jnp.where(high, both[:, :512], both[:, 512:]) + got.astype(jnp.float32)


def swap(array):
    return lax.ppermute(array, ("xh", "c"), TRANSPOSE)


def on_device(queries, key_rows, values, upstream, out_weight, doc_lengths):
    xs, xh = lax.axis_index("xs"), lax.axis_index("xh")
    first = pack(queries, key_rows, values, 0)
    group_rows, first = lax.optimization_barrier((swap(upstream[0]), first))
    first = exchange(first)
    tok_rows = lax.all_gather(group_rows, ("z", "c"), axis=0, tiled=True)

    second = pack(queries, key_rows, values, 1)
    second, out_weight, group_rows = lax.optimization_barrier((second, out_weight, group_rows))
    second = swap(second)
    weight = lax.all_gather(out_weight, ("y", "c"), axis=1, tiled=True)
    second, weight = lax.optimization_barrier((second, weight))
    weight = lax.ppermute(weight, ("xs", "c"), TRANSPOSE)
    lengths = lax.dynamic_index_in_dim(doc_lengths[0], xs, 0, keepdims=False)
    lengths = swap(lengths)
    ends = jnp.cumsum(lengths)
    shift = jnp.sum(jnp.where(lengths == HALF, ends - HALF, 0), dtype=jnp.int32)
    info = jnp.concatenate([jnp.stack([xh.astype(jnp.int32), shift]), ends])
    first, weight, info = lax.optimization_barrier((first, weight, info))
    other_weight = lax.ppermute(weight, "xh", SWAP)
    second, first, other_weight = lax.optimization_barrier((second, first, other_weight))
    other = lax.ppermute(take_other(info, first), "xh", SWAP)
    second = exchange(second)

    weights = jnp.concatenate(
        [jnp.where(xh == 0, weight, other_weight), jnp.where(xh == 0, other_weight, weight)]
    )
    grad_attn = project(tok_rows, weights)
    grads, out = attend(info, first, other, grad_attn, 0)
    term = weight_term(out, tok_rows)
    grads, second, term = lax.optimization_barrier((grads, second, term))
    sums = [sum_planes(term)]
    grads = exchange(grads)
    near, far, out = attend(info, second, second, grad_attn, 1)
    back = put_other(info, lax.ppermute(far, "xh", SWAP), near)
    term = weight_term(out, tok_rows)
    back, grads, term, sums = lax.optimization_barrier((back, grads, term, sums))
    back = exchange(back)
    grads = swap(grads)
    grads, sums = lax.optimization_barrier((grads, [*sums, sum_planes(term)]))

    send = jnp.where(xh == 0, sums[1], sums[0]).astype(jnp.bfloat16)
    total = jnp.where(xh == 0, sums[0], sums[1]) + lax.ppermute(send, "xh", SWAP).astype(jnp.float32)
    one, two = total[:, :256], total[:, 256:]
    straight = lax.ppermute(jnp.where(xs == 0, one, two), ("xs", "c"), TRANSPOSE)
    crossed = lax.ppermute(
        jnp.where(xs == 0, two, one), ("xs", "c"), [(0, 1), (1, 3), (2, 0), (3, 2)]
    )
    grad_weight = straight + crossed
    held = unpack(grads, 0, ())
    held = unpack(back, 1, held)
    return (*held, grad_weight)


def solution(mesh):
    fine = Mesh(mesh.devices.reshape(2, 2, ZN, 4, 2), ("xs", "xh", "z", "y", "c"))
    ctx, dp = ("xs", "xh", "z"), ("y", "c")
    rows = P(dp, ctx, None)
    return jax.shard_map(
        on_device,
        mesh=fine,
        in_specs=(rows, rows, rows, rows, P(ctx, dp), P(dp, None, None)),
        out_specs=(rows, rows, rows, P(ctx, dp)),
        check_vma=False,
    )
```

```python
import jax
import jax.numpy as jnp
from jax import lax
from jax.experimental import pallas as pl
from jax.experimental.pallas import tpu as pltpu
from jax.sharding import Mesh, PartitionSpec as P

HD = 128
SEQS = 2
ZN = 8
TILE = 128
SEQ = 2048
HALF = SEQ // 2
BLK = 1024
SWAP = [(0, 1), (1, 0)]
TRANSPOSE = [(0, 0), (1, 2), (2, 1), (3, 3)]
LOW = -1e30
VMEM_LIMIT = 48 * 1024 * 1024


def params(limit=VMEM_LIMIT):
    return pltpu.CompilerParams(vmem_limit_bytes=limit)


def matmul(lhs, rhs, left, right):
    return lax.dot_general(
        lhs, rhs, (((left,), (right,)), ((), ())), preferred_element_type=jnp.float32
    )


def pack_kernel(q_ref, k_ref, v_ref, out_ref):
    for z in range(ZN):
        for t, ref in enumerate((q_ref, k_ref, v_ref)):
            out_ref[z, 0, t * TILE : (t + 1) * TILE, :] = ref[0, :, z * HD : (z + 1) * HD]


def pack(queries, keys, values, chunk):
    rows = pl.BlockSpec((1, TILE, ZN * HD), lambda c: (0, 0, 2 * c + chunk))
    return pl.pallas_call(
        pack_kernel,
        grid=(2,),
        in_specs=[rows] * 3,
        out_specs=pl.BlockSpec((ZN, 1, 3 * TILE, HD), lambda c: (0, c, 0, 0)),
        out_shape=jax.ShapeDtypeStruct((ZN, 2, 3 * TILE, HD), jnp.bfloat16),
        compiler_params=params(60 * 1024 * 1024),
        name=f"pack{chunk}",
    )(queries, keys, values)


def unpack_kernel(in_ref, *refs):
    for z in range(ZN):
        for t, ref in enumerate(refs[-3:]):
            ref[0, :, z * HD : (z + 1) * HD] = in_ref[z, 0, t * TILE : (t + 1) * TILE, :]


def unpack(blocks, chunk, held):
    rows = pl.BlockSpec((1, TILE, ZN * HD), lambda c: (0, 0, 2 * c + chunk))
    whole = jax.ShapeDtypeStruct((1, TILE, 4 * ZN * HD), jnp.bfloat16)
    return pl.pallas_call(
        unpack_kernel,
        grid=(2,),
        in_specs=[pl.BlockSpec((ZN, 1, 3 * TILE, HD), lambda c: (0, c, 0, 0))]
        + [pl.BlockSpec(memory_space=pl.ANY)] * len(held),
        out_specs=[rows] * 3,
        out_shape=[whole] * 3,
        input_output_aliases={i + 1: i for i in range(len(held))},
        compiler_params=params(),
        name=f"unpack{chunk}",
    )(blocks, *held)


def take_kernel(info_ref, in_ref, out_ref):
    out_ref[...] = in_ref[...]


def take_other(info, blocks):
    half = (ZN, 1, 3 * TILE, HD)
    return pl.pallas_call(
        take_kernel,
        grid_spec=pltpu.PrefetchScalarGridSpec(
            num_scalar_prefetch=1,
            grid=(1,),
            in_specs=[pl.BlockSpec(half, lambda i, info: (0, 1 - info[0], 0, 0))],
            out_specs=pl.BlockSpec(half, lambda i, info: (0, 0, 0, 0)),
        ),
        out_shape=jax.ShapeDtypeStruct(half, jnp.bfloat16),
        compiler_params=params(),
        name="take",
    )(info, blocks)


def put_kernel(info_ref, in_ref, held_ref, out_ref):
    out_ref[...] = in_ref[...]


def put_other(info, part, blocks):
    return pl.pallas_call(
        put_kernel,
        grid_spec=pltpu.PrefetchScalarGridSpec(
            num_scalar_prefetch=1,
            grid=(1,),
            in_specs=[
                pl.BlockSpec((ZN, 1, 3 * TILE, HD), lambda i, info: (0, 0, 0, 0)),
                pl.BlockSpec(memory_space=pl.ANY),
            ],
            out_specs=pl.BlockSpec((ZN, 1, 3 * TILE, HD), lambda i, info: (0, 1 - info[0], 0, 0)),
        ),
        out_shape=jax.ShapeDtypeStruct((ZN, 2, 3 * TILE, HD), jnp.bfloat16),
        input_output_aliases={2: 0},
        compiler_params=params(60 * 1024 * 1024),
        name="put",
    )(info, part, blocks)


def attend_kernel(info, one, two, g, *refs):
    *grads_out, o_out, q_s, k_s, v_s, g_s, kt_s, vt_s, b_q, b_k, b_v, b_o = refs
    factor = HD ** (-0.5)
    shift = info[1]
    tiles = SEQ // TILE
    sides = (info[0], 1 - info[0])
    in_sides, out_sides = (sides, (0, 1)) if len(grads_out) == 1 else ((0, 1), sides)

    def wrap(row):
        return jnp.where(row < 0, row + SEQ, jnp.where(row >= SEQ, row - SEQ, row))

    def repeat(buf):
        buf[SEQ:, :] = buf[:TILE, :]

    for side, part in zip(in_sides, (one, two)):
        for z in range(ZN):
            rows = pl.ds(pl.multiple_of(side * HALF + z * TILE, TILE), TILE)
            for t, buf in enumerate((b_q, b_k, b_v)):
                buf[rows, :] = part[z, 0, t * TILE : (t + 1) * TILE, :].astype(jnp.float32)
    for z in range(ZN):
        for c in range(2):
            row = c * HALF + z * TILE
            b_o[row : row + TILE, :] = g[z, c].astype(jnp.float32)
    for buf, ref in ((b_q, q_s), (b_k, k_s), (b_v, v_s), (b_o, g_s)):
        repeat(buf)
        for j in range(tiles):
            rows = pl.ds(wrap(shift + j * TILE), TILE)
            ref[j * TILE : (j + 1) * TILE, :] = buf[rows, :].astype(jnp.bfloat16)
    for n in range(2):
        kt_s[n] = k_s[n * HALF : (n + 1) * HALF, :].T
        vt_s[n] = v_s[n * HALF : (n + 1) * HALF, :].T
    b_k[...] = jnp.zeros_like(b_k)
    b_v[...] = jnp.zeros_like(b_v)
    ends = [wrap(info[2 + d] - shift) for d in range(8)]

    for n in range(2):
        low = n * HALF
        keys = slice(low, low + HALF)

        def query_block(i, carry):
            rows = pl.ds(pl.multiple_of(low + i * BLK, BLK), BLK)
            q_i, g_i = q_s[rows, :], g_s[rows, :]
            s = matmul(k_s[keys, :], q_i, 1, 1)
            if n == 1:
                place = low + i * BLK + lax.broadcasted_iota(jnp.int32, (1, BLK), 1)
                start, stop = jnp.full_like(place, HALF), jnp.full_like(place, SEQ)
                for end in ends:
                    start = jnp.maximum(start, jnp.where(end <= place, end, HALF))
                    stop = jnp.minimum(stop, jnp.where(end > place, end, SEQ))
                seen = low + lax.broadcasted_iota(jnp.int32, (HALF, BLK), 0)
                s = jnp.where((seen >= start) & (seen < stop), s, LOW)
            top = jnp.max(s, axis=0, keepdims=True)
            probs = jnp.exp((s - top) * factor)
            probs = probs * (1.0 / jnp.sum(probs, axis=0, keepdims=True))
            probs_low = probs.astype(jnp.bfloat16)
            out = matmul(vt_s[n], probs_low, 1, 0).astype(jnp.bfloat16).astype(jnp.float32)
            delta = jnp.sum(g_i.astype(jnp.float32).T * out, axis=0, keepdims=True)
            b_o[rows, :] = out.T
            grad_p = matmul(v_s[keys, :], g_i, 1, 1)
            grad_s = (probs * (grad_p - delta)).astype(jnp.bfloat16)
            b_v[keys, :] += matmul(probs_low, g_i, 1, 0)
            b_k[keys, :] += matmul(grad_s, q_i, 1, 0)
            b_q[rows, :] = (matmul(kt_s[n], grad_s, 1, 0) * factor).T
            return carry

        lax.fori_loop(0, HALF // BLK, query_block, 0)

    for buf in (b_q, b_k, b_v, b_o):
        repeat(buf)
    for z in range(ZN):
        for n, side in enumerate(out_sides):
            ref, at = (grads_out[0], n) if len(grads_out) == 1 else (grads_out[n], 0)
            rows = pl.ds(wrap(side * HALF + z * TILE - shift), TILE)
            ref[z, at, :TILE, :] = b_q[rows, :].astype(jnp.bfloat16)
            ref[z, at, TILE : 2 * TILE, :] = (b_k[rows, :] * factor).astype(jnp.bfloat16)
            ref[z, at, 2 * TILE :, :] = b_v[rows, :].astype(jnp.bfloat16)
        for c in range(2):
            rows = pl.ds(wrap(c * HALF + z * TILE - shift), TILE)
            o_out[z, c] = b_o[rows, :].astype(jnp.bfloat16)


def attend(info, one, two, grad_attn, chunk):
    flat = (SEQ, HD)
    whole, half = (ZN, 2, 3 * TILE, HD), (ZN, 1, 3 * TILE, HD)
    first = pl.BlockSpec(half, lambda i, info: (0, 0, 0, 0))
    if chunk == 0:
        in_specs = [pl.BlockSpec(half, lambda i, info: (0, info[0], 0, 0)), first]
        out_specs = [pl.BlockSpec(whole, lambda i, info: (0, 0, 0, 0))]
        shapes = [whole]
    else:
        in_specs = [first, pl.BlockSpec(half, lambda i, info: (0, 1, 0, 0))]
        out_specs = [pl.BlockSpec(half, lambda i, info: (0, info[0], 0, 0)), first]
        shapes = [whole, half]
    return pl.pallas_call(
        attend_kernel,
        grid_spec=pltpu.PrefetchScalarGridSpec(
            num_scalar_prefetch=1,
            grid=(1,),
            in_specs=in_specs
            + [pl.BlockSpec((ZN, 2, TILE, HD), lambda i, info: (0, 0, 0, chunk))],
            out_specs=out_specs + [pl.BlockSpec((ZN, 2, TILE, HD), lambda i, info: (0, 0, 0, 0))],
            scratch_shapes=[pltpu.VMEM(flat, jnp.bfloat16)] * 4
            + [pltpu.VMEM((2, HD, HALF), jnp.bfloat16)] * 2
            + [pltpu.VMEM((SEQ + TILE, HD), jnp.float32)] * 4,
        ),
        out_shape=[jax.ShapeDtypeStruct(s, jnp.bfloat16) for s in shapes + [(ZN, 2, TILE, HD)]],
        compiler_params=params(),
        cost_estimate=pl.CostEstimate(
            flops=24 * SEQ * SEQ * HD, bytes_accessed=8 << 20, transcendentals=SEQ * SEQ // 2
        ),
        name=f"attend{chunk}",
    )(info, one, two, grad_attn)


def project_kernel(rows_ref, weight_ref, out_ref):
    out = matmul(rows_ref[...], weight_ref[...], 1, 1).astype(jnp.bfloat16)
    for n in range(out.shape[0] // TILE):
        out_ref[n // 2, n % 2] = out[n * TILE : (n + 1) * TILE]


def project(rows, weights):
    width = rows.shape[1]
    return pl.pallas_call(
        project_kernel,
        grid=(SEQ // BLK,),
        in_specs=[
            pl.BlockSpec((BLK, width), lambda i: (i, 0)),
            pl.BlockSpec((2 * HD, width), lambda i: (0, 0)),
        ],
        out_specs=pl.BlockSpec((BLK // TILE // 2, 2, TILE, 2 * HD), lambda i: (i, 0, 0, 0)),
        out_shape=jax.ShapeDtypeStruct((ZN, 2, TILE, 2 * HD), jnp.bfloat16),
        compiler_params=params(),
        cost_estimate=pl.CostEstimate(
            flops=4 * SEQ * HD * width, bytes_accessed=10 << 20, transcendentals=0
        ),
        name="project",
    )(rows, weights)


def exchange(blocks):
    flat = blocks.reshape(2 * ZN, 3 * TILE, HD)
    moved = lax.all_to_all(flat, ("z", "c"), split_axis=0, concat_axis=0, tiled=True)
    return moved.reshape(blocks.shape)


def weight_term(out, rows):
    return jnp.einsum(
        "tf,tc->fc", out.reshape(SEQ, HD), rows, preferred_element_type=jnp.float32
    )


def sum_planes(term):
    y = lax.axis_index("y")
    low, high = lax.bitwise_and(y, 1) == 0, y < 2
    parts = [term[:, i * 512 : (i + 1) * 512] for i in range(4)]
    even = jnp.concatenate([parts[0], parts[2]], axis=1)
    odd = jnp.concatenate([parts[1], parts[3]], axis=1)
    send = jnp.where(low, odd, even).astype(jnp.bfloat16)
    got = lax.ppermute(send, "y", [(0, 1), (1, 0), (2, 3), (3, 2)])
    both = jnp.where(low, even, odd) + got.astype(jnp.float32)
    send = jnp.where(high, both[:, 512:], both[:, :512]).astype(jnp.bfloat16)
    got = lax.ppermute(send, "y", [(0, 2), (2, 0), (1, 3), (3, 1)])
    return jnp.where(high, both[:, :512], both[:, 512:]) + got.astype(jnp.float32)


def swap(array):
    return lax.ppermute(array, ("xh", "c"), TRANSPOSE)


def on_device(queries, key_rows, values, upstream, out_weight, doc_lengths):
    xs, xh = lax.axis_index("xs"), lax.axis_index("xh")
    first = pack(queries, key_rows, values, 0)
    group_rows, first = lax.optimization_barrier((swap(upstream[0]), first))
    first = exchange(first)
    tok_rows = lax.all_gather(group_rows, ("z", "c"), axis=0, tiled=True)

    second = pack(queries, key_rows, values, 1)
    second, out_weight, group_rows = lax.optimization_barrier((second, out_weight, group_rows))
    second = swap(second)
    weight = lax.all_gather(out_weight, ("y", "c"), axis=1, tiled=True)
    second, weight = lax.optimization_barrier((second, weight))
    weight = lax.ppermute(weight, ("xs", "c"), TRANSPOSE)
    lengths = lax.dynamic_index_in_dim(doc_lengths[0], xs, 0, keepdims=False)
    lengths = swap(lengths)
    ends = jnp.cumsum(lengths)
    shift = jnp.sum(jnp.where(lengths == HALF, ends - HALF, 0), dtype=jnp.int32)
    info = jnp.concatenate([jnp.stack([xh.astype(jnp.int32), shift]), ends])
    first, weight, info = lax.optimization_barrier((first, weight, info))
    rows = HD - 16
    most = lax.ppermute(weight[:rows], "xh", SWAP)
    second, first, most, weight = lax.optimization_barrier((second, first, most, weight))
    other_weight = jnp.concatenate([most, lax.ppermute(weight[rows:], "xh", SWAP)])
    other = lax.ppermute(take_other(info, first), "xh", SWAP)
    second = exchange(second)

    weights = jnp.concatenate(
        [jnp.where(xh == 0, weight, other_weight), jnp.where(xh == 0, other_weight, weight)]
    )
    grad_attn = project(tok_rows, weights)
    grads, out = attend(info, first, other, grad_attn, 0)
    term = weight_term(out, tok_rows)
    grads, second, term = lax.optimization_barrier((grads, second, term))
    sums = [sum_planes(term)]
    grads = exchange(grads)
    near, far, out = attend(info, second, second, grad_attn, 1)
    back = put_other(info, lax.ppermute(far, "xh", SWAP), near)
    term = weight_term(out, tok_rows)
    back, grads, term, sums = lax.optimization_barrier((back, grads, term, sums))
    back = exchange(back)
    grads = swap(grads)
    grads, sums = lax.optimization_barrier((grads, [*sums, sum_planes(term)]))

    send = jnp.where(xh == 0, sums[1], sums[0]).astype(jnp.bfloat16)
    total = jnp.where(xh == 0, sums[0], sums[1]) + lax.ppermute(send, "xh", SWAP).astype(jnp.float32)
    one, two = total[:, :256], total[:, 256:]
    straight = lax.ppermute(jnp.where(xs == 0, one, two), ("xs", "c"), TRANSPOSE)
    crossed = lax.ppermute(
        jnp.where(xs == 0, two, one), ("xs", "c"), [(0, 1), (1, 3), (2, 0), (3, 2)]
    )
    grad_weight = straight + crossed
    held = unpack(grads, 0, ())
    held = unpack(back, 1, held)
    return (*held, grad_weight)


def solution(mesh):
    fine = Mesh(mesh.devices.reshape(2, 2, ZN, 4, 2), ("xs", "xh", "z", "y", "c"))
    ctx, dp = ("xs", "xh", "z"), ("y", "c")
    rows = P(dp, ctx, None)
    return jax.shard_map(
        on_device,
        mesh=fine,
        in_specs=(rows, rows, rows, rows, P(ctx, dp), P(dp, None, None)),
        out_specs=(rows, rows, rows, P(ctx, dp)),
        check_vma=False,
    )
```
